256 devices in a mesh: row: 16 (over x_hi, z), col: 16 (over x_lo, y, core).
Axes of the slice: x: 4 (x_hi: 2, x_lo: 2; x = x_hi * 2 + x_lo), y: 4, z: 8, core: 2. Of those that a mesh axis runs over, the one named last changes fastest.
Arguments:
- features: bfloat16 [65536, 256], P(('col', 'row')), may hold values from -6 to 6
- block_values: bfloat16 [16, 16, 32, 128, 128], P('row', 'col'), may hold values from -0.25 to 0.25
- block_rows: int32 [16, 16, 32], P('row', 'col'), may hold values from 0 to 31, as said below
- block_cols: int32 [16, 16, 32], P('row', 'col'), may hold values from 0 to 31
- block_count: int32 [16, 16], P('row', 'col'), may hold values from 2 to 32, as said below
- weight_in: bfloat16 [256, 1024], replicated, may hold values from -0.375 to 0.375
- weight_out: bfloat16 [1024, 256], replicated, may hold values from -0.1875 to 0.1875
- cotangent: bfloat16 [65536, 256], P(('row', 'col')), may hold values from -6 to 6
Outputs:
- layer_out: bfloat16 [65536, 256], P(('row', 'col'))
- grad_x: bfloat16 [65536, 256], P(('col', 'row'))
- grad_w_in: float32 [256, 1024], replicated
- grad_w_out: float32 [1024, 256], replicated
The draws below stay inside these ranges and needn't reach their ends.
Inputs may be any that keep to these rules, and one draw needn't show every extreme that they name: Within one device the slots name distinct blocks (pairs of block_rows and block_cols), live or not. `block_count`: one grid row, drawn from the seed, has 32 live slots on every device.
All inputs are finite; a program needn't handle non-finite values.
Results may differ from the reference program's by a relative error of at most 0.01.
Values may be sent and summed in bfloat16 or wider, within the bound.
A program may use at most 64 MiB of HBM per device.

```python
from functools import partial
import jax
import jax.numpy as jnp
from jax import lax

F = 256
HID = 1024
BLK = 128
NBMAX = 32
VERTS = 65536
RBLK = 32
CBLK = 32
N_ROW = 16
N_COL = 16


def block_places(key):
    keys = jax.random.split(key, N_ROW * N_COL)
    chosen = jax.vmap(lambda single: jax.random.permutation(single, RBLK * CBLK)[:NBMAX])(keys)
    return chosen.reshape(N_ROW, N_COL, NBMAX).astype(jnp.int32)


def draw_block_rows(key, part):
    places = block_places(key)
    return (places // CBLK).astype(jnp.int32)


def draw_block_cols(key, part):
    places = block_places(key)
    return (places % CBLK).astype(jnp.int32)


def draw_block_count(key, part):
    key = jax.random.fold_in(key, 7)
    heavy_key, light_key = jax.random.split(key)
    lowest = max(1, NBMAX // 16)
    highest = max(lowest + 1, NBMAX // 4 + 1)
    heavy_row = jax.random.randint(heavy_key, (), 0, N_ROW, dtype=jnp.int32)
    light = jax.random.randint(light_key, (N_ROW, N_COL), lowest, highest, dtype=jnp.int32)
    grid_rows = jnp.arange(N_ROW, dtype=jnp.int32)[:, None]
    return jnp.where(grid_rows == heavy_row, NBMAX, light).astype(jnp.int32)


def level_of(own_key, extent, cuts, least, high):
    factor_of, own = 1.0, jax.random.fold_in(own_key, 6)
    for position, parts in cuts:
        heights = jnp.exp(jax.random.uniform(jax.random.fold_in(own, position), (parts,), jnp.float32, least / len(cuts), high / len(cuts)))
        factor_of = factor_of * jnp.repeat(heights, extent[position] // parts).reshape([-1 if axis == position else 1 for axis in range(len(extent))])
    return factor_of


def noise(own_key, shape, width, most, shards=(), kind=jnp.bfloat16):
    entries = jax.random.normal(own_key, shape, jnp.float32) * width
    if len(shards) > 0:
        entries = level_of(own_key, shape, shards, -0.22, 0.18) * entries
    return jnp.clip(entries, min=-most, max=most).astype(kind)


def setup_inputs(seed: int = 0) -> dict:
    arg_keys = jax.random.split(jax.random.key(seed), 9)
    return {
        "features": noise(arg_keys[0], (VERTS, F), 1.0, 6.0, ((0, 256),)),
        "block_values": noise(arg_keys[1], (N_ROW, N_COL, NBMAX, BLK, BLK), (4 * BLK) ** -0.5, 0.25, ((0, 16), (1, 16))),
        "block_rows": draw_block_rows(jax.random.fold_in(arg_keys[8], 71), 0),
        "block_cols": draw_block_cols(jax.random.fold_in(arg_keys[8], 71), 0),
        "block_count": draw_block_count(jax.random.fold_in(arg_keys[8], 71), 0),
        "weight_in": noise(arg_keys[5], (F, HID), F ** -0.5, 0.375),
        "weight_out": noise(arg_keys[6], (HID, F), HID ** -0.5, 0.1875),
        "cotangent": noise(arg_keys[7], (VERTS, F), 1.0, 6.0, ((0, 256),)),
    }


def reference(features, block_values, block_rows, block_cols, block_count, weight_in, weight_out, cotangent):
    slot_ids = jnp.arange(NBMAX, dtype=jnp.int32)
    live_mask = (slot_ids[None, None, :] < block_count[:, :, None]).astype(jnp.float32)
    feat_blocks = features.reshape(VERTS // BLK, BLK, F)
    col_global = (jnp.arange(N_COL, dtype=jnp.int32)[None, :, None] * CBLK + block_cols).astype(jnp.int32)
    row_global = (jnp.arange(N_ROW, dtype=jnp.int32)[:, None, None] * RBLK + block_rows).astype(jnp.int32)

    def row_group(packed):
        values, sources, targets, masks = packed
        taken = feat_blocks[sources.reshape(-1)]
        prod = jnp.einsum('sij,sjf->sif', values.reshape(-1, BLK, BLK).astype(jnp.float32), taken.astype(jnp.float32))
        prod = prod * masks.reshape(-1)[:, None, None]
        return jax.ops.segment_sum(prod, targets.reshape(-1), num_segments=RBLK).reshape(RBLK * BLK, F)
    pooled_full = lax.map(row_group, (block_values, col_global, block_rows, live_mask))
    pooled = pooled_full.reshape(VERTS, F).astype(jnp.bfloat16)
    pre_act = jnp.dot(pooled, weight_in, preferred_element_type=jnp.float32)
    gelu_fn = partial(jax.nn.gelu, approximate=True)
    activated = gelu_fn(pre_act).astype(jnp.bfloat16)
    layer_out = (pooled.astype(jnp.float32) + jnp.dot(activated, weight_out, preferred_element_type=jnp.float32)).astype(jnp.bfloat16)
    grad_act = jnp.dot(cotangent, weight_out.T, preferred_element_type=jnp.float32)
    grad_pre = jax.vjp(gelu_fn, pre_act)[1](grad_act)[0].astype(jnp.bfloat16)
    grad_pooled = (cotangent.astype(jnp.float32) + jnp.dot(grad_pre, weight_in.T, preferred_element_type=jnp.float32)).astype(jnp.bfloat16)
    grad_w_out = jnp.dot(activated.T, cotangent, preferred_element_type=jnp.float32)
    grad_w_in = jnp.dot(pooled.T, grad_pre, preferred_element_type=jnp.float32)
    grad_blocks = grad_pooled.reshape(VERTS // BLK, BLK, F)

    def col_group(packed):
        values, sources, targets, masks = packed
        taken = grad_blocks[sources.reshape(-1)]
        prod = jnp.einsum('sji,sjf->sif', values.reshape(-1, BLK, BLK).astype(jnp.float32), taken.astype(jnp.float32))
        prod = prod * masks.reshape(-1)[:, None, None]
        return jax.ops.segment_sum(prod, targets.reshape(-1), num_segments=CBLK).reshape(CBLK * BLK, F)
    grad_full = lax.map(col_group, (jnp.swapaxes(block_values, 0, 1), jnp.swapaxes(row_global, 0, 1), jnp.swapaxes(block_cols, 0, 1), jnp.swapaxes(live_mask, 0, 1)))
    grad_x = grad_full.reshape(VERTS, F).astype(jnp.bfloat16)
    return (layer_out, grad_x, grad_w_in, grad_w_out)
```

```python
import jax
import jax.numpy as jnp
from jax import lax
from jax.experimental import pallas as pl
from jax.experimental.pallas import tpu as pltpu
from jax.sharding import PartitionSpec as P

MESH = pl.DeviceIdType.MESH
F32, BF16 = jnp.float32, jnp.bfloat16
BLK, WIDTH, HID, SLOTS, BLOCKS = 128, 256, 1024, 32, 32
ROWS, COLS, PREV_F, PREV_B, LAST_F, LAST_B = range(6)


def dot(a, b, ca=1, cb=0):
    return lax.dot_general(a, b, (((ca,), (cb,)), ((), ())), preferred_element_type=F32)


def kernel(
    tab, count, feat, values_h, win_h, wout_h, cot_h,
    lout, gx, gwin, gwout,
    val, valt, win, wout, cot,
    feats, grads, scan, pstage, precv, qstage, qrecv, own,
    zstage, zrecv, xstage, xrecv, gpool,
    wacc, wstage, wrecv0, wsend1, wrecv1, wsum, wsend2, wrecv2, wsend3, wfull,
    sem_in, s_ag, r_ag, s_x, r_x, s_p, r_p, s_q, r_q, s_g, r_g, s_gf, r_gf,
    s_z, r_z, s_w, r_w, s_w1, r_w1, s_w2, r_w2, s_w3, r_w3, s_w4, r_w4, s_w5, r_w5,
):
    r, c = lax.axis_index("row"), lax.axis_index("col")
    xh, z = r // 8, r % 8
    j, k = c // 2, c % 2
    xl, y = j // 4, j % 4
    sibling = (r, 2 * j + 1 - k)

    def chip(m):
        return ((xl + m // 4) % 2) * 4 + (y + m % 4) % 4

    def behind(m):
        return ((xl + m // 4) % 2) * 4 + (y + 4 - m % 4) % 4

    def rank(n):
        return ((xh + n // 8) % 2) * 8 + (z + n % 8) % 8

    def remote(src, dst, ss, rs, to):
        return pltpu.make_async_remote_copy(
            src_ref=src, dst_ref=dst, send_sem=ss, recv_sem=rs, device_id=to, device_id_type=MESH
        )

    def each(lo, hi, f):
        lax.fori_loop(lo, hi, lambda i, _: (f(i), 0)[1], 0)

    loads = [
        pltpu.make_async_copy(a, b, sem_in.at[i])
        for i, (a, b) in enumerate(((values_h, val), (win_h, win), (wout_h, wout), (cot_h, cot)))
    ]
    for one in loads:
        one.start()

    barrier = pltpu.get_barrier_semaphore()
    pl.semaphore_signal(barrier, inc=1, device_id=sibling, device_id_type=MESH)
    each(1, 8, lambda m: pl.semaphore_signal(
        barrier, inc=1, device_id=(r, 2 * chip(m) + k), device_id_type=MESH))
    each(1, 16, lambda n: pl.semaphore_signal(
        barrier, inc=1, device_id=(rank(n), c), device_id_type=MESH))
    pl.semaphore_wait(barrier, 23)

    partner = ((1 - xh) * 8 + z, c)
    sign = (1, 7)
    ahead = [(xh * 8 + (z + g) % 8, c) for g in sign]

    def ag_copy(d, s, p):
        plane = (xh + p) % 2
        at = 2 * (plane * 8 + (z + (8 - sign[d]) * s) % 8)
        part = pl.ds(at, 2) if s < 3 else pl.ds(at + d, 1)
        src = feat if s == 0 and p == 0 else feats.at[part]
        return remote(src, feats.at[part], s_ag.at[d, s, p], r_ag.at[d, s, p], ahead[d])

    swap = remote(feat, feats.at[pl.ds(2 * r, 2)], s_x.at[0], r_x.at[0], partner)
    for d in (0, 1):
        ag_copy(d, 0, 0).start()
    swap.start()
    feats[pl.ds(2 * r, 2)] = feat[...]

    loads[0].wait()

    def mask(s):
        live = jnp.where(s < count[0], 1.0, 0.0).astype(F32)
        masked = val[s].astype(F32) * live
        val[s] = masked.astype(BF16)
        valt[s] = masked.T.astype(BF16)

    for s in range(4):
        for p in (0, 1):
            if s == 0 and p == 0:
                continue
            if s == 0:
                swap.wait_recv()
            for d in (0, 1):
                if s > 0:
                    ag_copy(d, s - 1, p).wait_recv()
                ag_copy(d, s, p).start()
        each(8 * s, 8 * s + 8, mask)
    for one in loads[1:]:
        one.wait()
    for d in (0, 1):
        for p in (0, 1):
            ag_copy(d, 3, p).wait_recv()

    def aggregate(vals, source, prev, data):
        scan[0] = jnp.zeros((BLK, WIDTH), F32)

        def some(g):
            for u in range(8):
                s = g * 8 + u
                scan[s + 1] = dot(vals[s], data[tab[source, s]]) + scan[tab[prev, s]]

        each(0, SLOTS // 8, some)

    aggregate(val, COLS, PREV_F, feats)

    def p_copy(m):
        return remote(pstage.at[m], precv.at[m], s_p.at[m], r_p.at[m], sibling)

    def q_copy(m):
        return remote(
            qstage.at[m], qrecv.at[m], s_q.at[m], r_q.at[m], (r, 2 * chip(m) + k))

    def give(i):
        m = (i + 1) % 8
        at = 2 * (2 * chip(m) + 1 - k)
        for h in (0, 1):
            pstage[m, h] = scan[tab[LAST_F, at + h]].astype(BF16)
        p_copy(m).start()

    each(0, 8, give)

    def pair_sum(m, h):
        return scan[tab[LAST_F, 2 * (2 * chip(m) + k) + h]] + precv[m, h].astype(F32)

    def spread(m):
        p_copy(m).wait_recv()
        for h in (0, 1):
            qstage[m, h] = pair_sum(m, h).astype(BF16)
        q_copy(m).start()

    each(1, 8, spread)
    p_copy(0).wait_recv()
    for h in (0, 1):
        own[h] = pair_sum(0, h)

    def collect(m):
        q_copy(m).wait_recv()
        for h in (0, 1):
            own[h] += qrecv[m, h].astype(F32)

    each(1, 8, collect)

    pooled = own[...].reshape(2 * BLK, WIDTH).astype(BF16)
    ct = cot[...]
    out = pooled.astype(F32)
    back = ct.astype(F32)
    a0, a1 = 0.7978845608028654, 0.044715
    for t in range(4):
        cut = pl.ds(t * 256, 256)
        w_in, w_out = win[:, cut], wout[cut, :]
        pre = dot(pooled, w_in)
        square = pre * pre
        th = jnp.tanh(a0 * (pre + a1 * (square * pre)))
        cdf = 0.5 * (1.0 + th)
        act = (pre * cdf).astype(BF16)
        slope = cdf + 0.5 * pre * (1.0 - th * th) * (a0 * (1.0 + 3.0 * a1 * square))
        gpre = (dot(ct, w_out, 1, 1) * slope).astype(BF16)
        out = out + dot(act, w_out)
        back = back + dot(gpre, w_in, 1, 1)
        g_out = dot(act, ct, 0, 0)
        g_in = dot(pooled, gpre, 0, 0)
        for h in (0, 1):
            wacc[pl.ds(h * 1024 + t * 256, 256), :] = g_out[:, h * 128:(h + 1) * 128]
            wacc[pl.ds(2048 + (2 * t + h) * 256, 256), :] = g_in[:, h * 128:(h + 1) * 128]
    lout[...] = out.astype(BF16)
    gpool[...] = back.astype(BF16).reshape(2, BLK, WIDTH)

    def g_copy(m):
        return remote(
            gpool, grads.at[pl.ds(2 * c, 2)], s_g.at[m], r_g.at[m], (r, 2 * chip(m) + k))

    def gf_copy(m):
        at = pl.ds(2 * (2 * behind(m) + k), 2)
        return remote(grads.at[at], grads.at[at], s_gf.at[m], r_gf.at[m], sibling)

    each(1, 8, lambda m: g_copy(m).start())
    grads[pl.ds(2 * c, 2)] = gpool[...]
    gf_copy(0).start()

    def wchunk(n):
        return wacc[pl.ds(256 * n, 256), :]

    def wgive(m):
        wstage[m] = wchunk(2 * chip(m) + 1 - k).astype(BF16)

    each(0, 8, wgive)
    w0 = remote(wstage, wrecv0, s_w.at[0], r_w.at[0], sibling)
    w0.start()

    def pass_on(m):
        g_copy(m).wait_recv()
        gf_copy(m).start()

    each(1, 8, pass_on)

    def w1_copy(m):
        return remote(
            wsend1.at[m], wrecv1.at[m], s_w1.at[m], r_w1.at[m], (r, 2 * chip(m) + k))

    w0.wait_recv()

    def wspread(m):
        wsend1[m] = (wchunk(2 * chip(m) + k) + wrecv0[m].astype(F32)).astype(BF16)
        w1_copy(m).start()

    each(1, 8, wspread)
    wsum[...] = wchunk(c) + wrecv0[0].astype(F32)

    each(0, 8, lambda m: gf_copy(m).wait_recv())
    aggregate(valt, ROWS, PREV_B, grads)

    def z_copy(d, s, p):
        part = pl.ds(0, 2) if s > 0 else pl.ds(d, 1)
        return remote(
            zstage.at[d, s, p, part], zrecv.at[d, s, p, part],
            s_z.at[d, s, p], r_z.at[d, s, p], ahead[d])

    def term(p, zz, h):
        return scan[tab[LAST_B, 2 * (((xh + p) % 2) * 8 + zz % 8) + h]]

    def z_step(s):
        for p in (1, 0):
            for d in (0, 1):
                target = z + sign[d] * (4 - s)
                if s > 0:
                    z_copy(d, s - 1, p).wait_recv()
                for h in (0, 1):
                    if s == 0 and h != d:
                        continue
                    v = term(p, target, h)
                    if s > 1 or (s == 1 and h == d):
                        v = v + zrecv[d, s - 1, p, h].astype(F32)
                    zstage[d, s, p, h] = v.astype(BF16)
                z_copy(d, s, p).start()

    z_step(0)

    def w2_copy(n):
        return remote(
            wsend2.at[rank(n)], wrecv2.at[n], s_w2.at[n], r_w2.at[n], (rank(n), c))

    def wcollect(m):
        w1_copy(m).wait_recv()
        wsum[...] += wrecv1[m].astype(F32)

    each(1, 8, wcollect)
    wsend2[...] = wsum[...].astype(BF16).reshape(16, 16, 128)
    each(1, 16, lambda n: w2_copy(n).start())

    z_step(1)

    place = pl.ds(pl.multiple_of(256 * c + 16 * r, 16), 16)

    def w3_copy(n):
        return remote(wsend3, wfull.at[place], s_w3.at[n], r_w3.at[n], (rank(n), c))

    def wadd(n, total):
        w2_copy(n).wait_recv()
        return total + wrecv2[n].astype(F32)

    piece = lax.fori_loop(1, 16, wadd, wsum[pl.ds(pl.multiple_of(16 * r, 16), 16), :])
    wsend3[...] = piece.astype(BF16)
    wfull[place, :] = wsend3[...]
    each(1, 16, lambda n: w3_copy(n).start())

    z_step(2)

    def chunk(n):
        return wfull.at[pl.ds(pl.multiple_of(256 * n, 256), 256)]

    def w4_copy(m):
        return remote(chunk(c), chunk(c), s_w4.at[m], r_w4.at[m], (r, 2 * chip(m) + k))

    def w5_copy(m):
        part = chunk(2 * behind(m) + k)
        return remote(part, part, s_w5.at[m], r_w5.at[m], sibling)

    each(1, 16, lambda n: w3_copy(n).wait_recv())
    each(1, 8, lambda m: w4_copy(m).start())
    w5_copy(0).start()

    z_step(3)

    def wpass(m):
        w4_copy(m).wait_recv()
        w5_copy(m).start()

    each(1, 8, wpass)

    def arrived(p, h):
        v = term(p, z, h)
        return v + zrecv[0, 3, p, h].astype(F32) + zrecv[1, 3, p, h].astype(F32)

    for d in (0, 1):
        z_copy(d, 3, 1).wait_recv()
    for h in (0, 1):
        xstage[h] = arrived(1, h).astype(BF16)
    last = remote(xstage, xrecv, s_x.at[1], r_x.at[1], partner)
    last.start()
    for d in (0, 1):
        z_copy(d, 3, 0).wait_recv()
    mine = [arrived(0, h) for h in (0, 1)]

    each(0, 8, lambda m: w5_copy(m).wait_recv())
    for h in (0, 1):
        gwout[:, h * 128:(h + 1) * 128] = wfull[pl.ds(h * 1024, 1024), :]
    for t in range(8):
        gwin[:, t * 128:(t + 1) * 128] = wfull[pl.ds(2048 + t * 256, 256), :]
    last.wait_recv()
    for h in (0, 1):
        gx[h] = (mine[h] + xrecv[h].astype(F32)).astype(BF16)

    swap.wait_send()
    last.wait_send()
    w0.wait_send()
    for d in (0, 1):
        for s in range(4):
            for p in (0, 1):
                ag_copy(d, s, p).wait_send()
                z_copy(d, s, p).wait_send()

    def drain(m):
        for f in (p_copy, gf_copy, w5_copy):
            f(m).wait_send()

    def drain_chips(m):
        for f in (q_copy, g_copy, w1_copy, w4_copy):
            f(m).wait_send()

    def drain_ranks(n):
        w2_copy(n).wait_send()
        w3_copy(n).wait_send()

    each(0, 8, drain)
    each(1, 8, drain_chips)
    each(1, 16, drain_ranks)


def tables(rows, cols):
    keys = jnp.stack([rows, cols])
    slot = jnp.arange(SLOTS, dtype=jnp.int32)
    same = keys[:, :, None] == keys[:, None, :]
    before = slot[None, :] < slot[:, None]
    prev = jnp.max(jnp.where(same & before, slot[None, None, :] + 1, 0), axis=2)
    block = jnp.arange(BLOCKS, dtype=jnp.int32)
    hit = keys[:, None, :] == block[None, :, None]
    last = jnp.max(jnp.where(hit, slot[None, None, :] + 1, 0), axis=2)
    return jnp.concatenate([keys, prev, last]).astype(jnp.int32)


def body(features, block_values, block_rows, block_cols, block_count, weight_in, weight_out, cot):
    tab = tables(block_rows[0, 0], block_cols[0, 0])
    vm = lambda *shape, t=BF16: pltpu.VMEM(shape, t)
    dma = lambda *shape: pltpu.SemaphoreType.DMA(shape)
    smem = pl.BlockSpec(memory_space=pltpu.SMEM)
    vmem = pl.BlockSpec(memory_space=pltpu.VMEM)
    anywhere = pl.BlockSpec(memory_space=pl.ANY)
    lout, gx, gwin, gwout = pl.pallas_call(
        kernel,
        out_shape=(
            jax.ShapeDtypeStruct((2 * BLK, WIDTH), BF16),
            jax.ShapeDtypeStruct((2, BLK, WIDTH), BF16),
            jax.ShapeDtypeStruct((WIDTH, HID), BF16),
            jax.ShapeDtypeStruct((HID, WIDTH), BF16),
        ),
        in_specs=[smem, smem, vmem] + [anywhere] * 4,
        out_specs=(vmem, vmem, vmem, vmem),
        scratch_shapes=[
            vm(SLOTS, BLK, BLK), vm(SLOTS, BLK, BLK), vm(WIDTH, HID), vm(HID, WIDTH),
            vm(2 * BLK, WIDTH),
            vm(BLOCKS, BLK, WIDTH), vm(BLOCKS, BLK, WIDTH), vm(SLOTS + 1, BLK, WIDTH, t=F32),
            vm(8, 2, BLK, WIDTH), vm(8, 2, BLK, WIDTH), vm(8, 2, BLK, WIDTH),
            vm(8, 2, BLK, WIDTH), vm(2, BLK, WIDTH, t=F32),
            vm(2, 4, 2, 2, BLK, WIDTH), vm(2, 4, 2, 2, BLK, WIDTH),
            vm(2, BLK, WIDTH), vm(2, BLK, WIDTH), vm(2, BLK, WIDTH),
            vm(4096, 128, t=F32), vm(8, 256, 128), vm(8, 256, 128), vm(8, 256, 128),
            vm(8, 256, 128), vm(256, 128, t=F32), vm(16, 16, 128), vm(16, 16, 128),
            vm(16, 128), vm(4096, 128),
            dma(4), dma(2, 4, 2), dma(2, 4, 2), dma(2), dma(2), dma(8), dma(8), dma(8), dma(8),
            dma(8), dma(8), dma(8), dma(8), dma(2, 4, 2), dma(2, 4, 2), dma(1), dma(1),
            dma(8), dma(8), dma(16), dma(16), dma(16), dma(16), dma(8), dma(8), dma(8), dma(8),
        ],
        compiler_params=pltpu.CompilerParams(
            collective_id=0, has_side_effects=True, vmem_limit_bytes=52 * 2**20
        ),
        name="layer",
    )(
        tab, block_count[0], features.reshape(2, BLK, WIDTH), block_values[0, 0],
        weight_in, weight_out, cot,
    )
    return lout, gx.reshape(2 * BLK, WIDTH), gwin.astype(F32), gwout.astype(F32)


def solution(mesh):
    return jax.shard_map(
        body,
        mesh=mesh,
        in_specs=(
            P(("col", "row"), None),
            P("row", "col", None, None, None),
            P("row", "col", None),
            P("row", "col", None),
            P("row", "col"),
            P(),
            P(),
            P(("row", "col"), None),
        ),
        out_specs=(P(("row", "col"), None), P(("col", "row"), None), P(), P()),
        check_vma=False,
    )
```

```python
import jax
import jax.numpy as jnp
from jax import lax
from jax.experimental import pallas as pl
from jax.experimental.pallas import tpu as pltpu
from jax.sharding import PartitionSpec as P

MESH = pl.DeviceIdType.MESH
F32, BF16 = jnp.float32, jnp.bfloat16
BLK, HALF, WIDTH, HID, SLOTS, BLOCKS = 128, 128, 256, 1024, 32, 32


def dot(a, b, ca=1, cb=0):
    return lax.dot_general(a, b, (((ca,), (cb,)), ((), ())), preferred_element_type=F32)


def kernel(
    rows_h, cols_h, count_h, feat_h, values_h, win_h, wout_h, cot_h,
    lout, gx, gwin, gwout,
    rows, cols, count, prev_f, prev_b, last_f, last_b,
    val, valt, win, wout, cot, louts, gxs,
    feats0, feats1, grads0, grads1, scan, pstage, precv, qstage, qrecv, own,
    zstage, zrecv, xstage, xrecv, gpool,
    wacc, wstage, wrecv0, wsend1, wrecv1, wsum, wsend2, wrecv2, wsend3, wfull,
    sem_in, sem_out, s_ag, r_ag, r_x, r_y, s_p, r_p, s_q, r_q, s_g, r_g, s_gf, r_gf,
    s_z, r_z, s_w, r_w,
):
    feats, grads = (feats0, feats1), (grads0, grads1)
    r, c = lax.axis_index("row"), lax.axis_index("col")
    xh, z = r // 8, r % 8
    j, k = c // 2, c % 2
    xl, y = j // 4, j % 4
    sibling = (r, 2 * j + 1 - k)

    def chip(m):
        return ((xl + m // 4) % 2) * 4 + (y + m % 4) % 4

    def behind(m):
        return ((xl + m // 4) % 2) * 4 + (y + 4 - m % 4) % 4

    def along(n):
        return (xh * 8 + (z + n) % 8, c)

    x = 2 * xh + xl

    def spot(n):
        return ((x + n // 4) % 4) * 4 + (y + n % 4) % 4

    def level(q):
        return ((q // 8) * 8 + z, ((q // 4) % 2) * 8 + (q % 4) * 2 + k)

    partner = ((1 - xh) * 8 + z, c)
    sign = (1, 7)
    ahead = [(xh * 8 + (z + g) % 8, c) for g in sign]
    across = [((1 - xh) * 8 + (z + g) % 8, c) for g in sign]

    def remote(src, dst, ss, rs, to):
        return pltpu.make_async_remote_copy(
            src_ref=src, dst_ref=dst, send_sem=ss, recv_sem=rs, device_id=to, device_id_type=MESH
        )

    def take(view, sem):
        pltpu.make_async_copy(view, view, sem).wait()

    def each(lo, hi, f):
        lax.fori_loop(lo, hi, lambda i, _: (f(i), 0)[1], 0)

    halves = [pl.ds(0, HALF), pl.ds(HALF, HALF)]
    pairs = [(feat_h.at[:, :, halves[f]], feats[f].at[pl.ds(2 * r, 2)]) for f in (0, 1)]
    pairs += [(count_h, count), (rows_h, rows), (cols_h, cols), (values_h, val)]
    pairs += [(win_h, win), (wout_h, wout), (cot_h, cot)]
    loads = [pltpu.make_async_copy(a, b, sem_in.at[i]) for i, (a, b) in enumerate(pairs)]
    for one in loads[:5]:
        one.start()

    barrier = pltpu.get_barrier_semaphore()

    def greet(to):
        pl.semaphore_signal(barrier, inc=1, device_id=to, device_id_type=MESH)

    greet(sibling)
    each(1, 16, lambda n: greet(level(spot(n))))
    each(1, 8, lambda n: greet(along(n)))
    for one in across:
        greet(one)
    pl.semaphore_wait(barrier, 25)

    def ag_copy(f, d, s, p):
        plane = (xh + (p if s > 0 else 0)) % 2
        at = 2 * (plane * 8 + (z + (8 - sign[d]) * s) % 8)
        part = feats[f].at[pl.ds(at, 2) if s < 3 else pl.ds(at + d, 1)]
        to = across[d] if s == 0 and p == 1 else ahead[d]
        return remote(part, part, s_ag.at[f], r_ag.at[f, d, s, p], to)

    def swap(f):
        part = feats[f].at[pl.ds(2 * r, 2)]
        return remote(part, part, s_ag.at[f], r_x.at[f], partner)

    for f in (0, 1):
        loads[f].wait()
        for p in (0, 1):
            for d in (0, 1):
                ag_copy(f, d, 0, p).start()

    for one in loads[5:]:
        one.start()
    for one in loads[2:6]:
        one.wait()

    def mask(s):
        live = jnp.where(s < count[0, 0], 1.0, 0.0).astype(F32)
        masked = val[s].astype(F32) * live
        val[s] = masked.astype(BF16)
        valt[s] = masked.T.astype(BF16)

    def lists(s):
        for keys, prev, last in ((rows, prev_f, last_f), (cols, prev_b, last_b)):
            mine = keys[0, 0, s]
            before, newest = jnp.int32(0), jnp.int32(0)
            for t in range(SLOTS):
                before = jnp.where((keys[0, 0, t] == mine) & (t < s), t + 1, before)
                newest = jnp.where(keys[0, 0, t] == s, t + 1, newest)
            prev[s] = before
            last[s] = newest

    def pass_features(f, s, p):
        for d in (0, 1):
            ag_copy(f, d, s - 1, p).wait_recv()
            ag_copy(f, d, s, p).start()

    each(0, 16, mask)
    pass_features(0, 1, 0)
    pass_features(1, 1, 0)
    each(16, 32, mask)
    pass_features(0, 1, 1)
    for f in (0, 1):
        swap(f).start()
    pass_features(0, 2, 0)
    pass_features(1, 1, 1)
    pass_features(1, 2, 0)
    each(0, 12, lists)
    pass_features(0, 2, 1)
    pass_features(0, 3, 0)
    each(12, 24, lists)
    pass_features(1, 2, 1)
    pass_features(1, 3, 0)
    each(24, 32, lists)
    pass_features(0, 3, 1)
    for one in loads[6:]:
        one.wait()
    pass_features(1, 3, 1)

    def ag_wait(f):
        swap(f).wait_recv()
        for d in (0, 1):
            for p in (0, 1):
                ag_copy(f, d, 3, p).wait_recv()

    def aggregate(f, vals, source, prev, block):
        scan[f, 0] = jnp.zeros((BLK, HALF), F32)

        def some(g):
            for u in range(8):
                s = g * 8 + u
                scan[f, s + 1] = dot(vals[s], block(f, source[0, 0, s])) + scan[f, prev[s]]

        each(0, SLOTS // 8, some)

    def p_copy(f, g):
        part = pl.ds(4 * g, 4)
        return remote(
            pstage.at[f, part], precv.at[f, part], s_p.at[f, g], r_p.at[f, g], sibling)

    def q_copy(f, m):
        return remote(
            qstage.at[f, m - 1], qrecv.at[f, m - 1], s_q.at[f], r_q.at[f],
            (r, 2 * chip(m) + k))

    def give(f):
        for g in (0, 1):
            def one(i):
                at = 2 * (2 * chip((i + 1) % 8) + 1 - k)
                for h in (0, 1):
                    pstage[f, i, h] = scan[f, last_f[at + h]].astype(BF16)

            each(4 * g, 4 * g + 4, one)
            p_copy(f, g).start()

    def spread(f):
        def pair_sum(i, h):
            mine = scan[f, last_f[2 * (2 * chip((i + 1) % 8) + k) + h]]
            return mine + precv[f, i, h].astype(F32)

        def one(i):
            for h in (0, 1):
                qstage[f, i, h] = pair_sum(i, h).astype(BF16)
            q_copy(f, i + 1).start()

        p_copy(f, 0).wait_recv()
        each(0, 4, one)
        p_copy(f, 1).wait_recv()
        each(4, 7, one)
        for h in (0, 1):
            own[f, h] = pair_sum(7, h)

    def collect(f):
        take(qrecv.at[f], r_q.at[f])
        for h in (0, 1):
            total = own[f, h]
            for m in range(7):
                total += qrecv[f, m, h].astype(F32)
            own[f, h] = total

    for f in (0, 1):
        ag_wait(f)
        aggregate(f, val, cols, prev_f, lambda f, i: feats[f][i])
        give(f)
        spread(f)
    for f in (0, 1):
        collect(f)

    pooled = jnp.concatenate(
        [own[f].reshape(2 * BLK, HALF).astype(BF16) for f in (0, 1)], axis=1)
    ct = cot[...]
    out = pooled.astype(F32)
    back = ct.astype(F32)
    a0, a1 = 0.7978845608028654, 0.044715
    for t in range(4):
        cut = pl.ds(t * 256, 256)
        w_in, w_out = win[:, cut], wout[cut, :]
        pre = dot(pooled, w_in)
        square = pre * pre
        th = jnp.tanh(a0 * (pre + a1 * (square * pre)))
        cdf = 0.5 * (1.0 + th)
        act = (pre * cdf).astype(BF16)
        slope = cdf + 0.5 * pre * (1.0 - th * th) * (a0 * (1.0 + 3.0 * a1 * square))
        gpre = (dot(ct, w_out, 1, 1) * slope).astype(BF16)
        out = out + dot(act, w_out)
        back = back + dot(gpre, w_in, 1, 1)
        g_out = dot(act, ct, 0, 0)
        g_in = dot(pooled, gpre, 0, 0)
        for h in (0, 1):
            wacc[pl.ds(h * 1024 + t * 256, 256), :] = g_out[:, h * 128:(h + 1) * 128]
            wacc[pl.ds(2048 + (2 * t + h) * 256, 256), :] = g_in[:, h * 128:(h + 1) * 128]
    louts[...] = out.astype(BF16)
    stores = [pltpu.make_async_copy(louts, lout, sem_out.at[0])]
    stores[0].start()
    for f in (0, 1):
        gpool[f] = back[:, f * HALF:(f + 1) * HALF].astype(BF16).reshape(2, BLK, HALF)

    def g_copy(f, m):
        return remote(
            gpool.at[f], grads[f].at[j, k], s_g.at[f], r_g.at[f], (r, 2 * chip(m) + k))

    def gf_copy(f):
        part = grads[f].at[:, k]
        return remote(part, part, s_gf.at[f], r_gf.at[f], sibling)

    for f in (0, 1):
        each(1, 8, lambda m: g_copy(f, m).start())
    for f in (0, 1):
        grads[f][j, k] = gpool[f]

    wstage[...] = wacc[pl.ds(2048 * (1 - k), 2048), :].astype(BF16)
    w0 = remote(wstage, wrecv0, s_w.at[0], r_w.at[0], sibling)
    w0.start()

    def w1_copy(n):
        return remote(wsend1.at[n - 1], wrecv1.at[n - 1], s_w.at[1], r_w.at[1], along(n))

    def w2_copy(n):
        q = spot(n)
        return remote(wsend2.at[q], wrecv2.at[n - 1], s_w.at[2], r_w.at[2], level(q))

    def w3_copy(n):
        return remote(
            wsend3, wfull.at[k * 8 + z, spot(0)], s_w.at[3], r_w.at[3], along(n))

    def w4_copy(n):
        part = wfull.at[pl.ds(k * 8, 8), spot(0)]
        return remote(part, part, s_w.at[4], r_w.at[4], level(spot(n)))

    def two_cores(n):
        at = pl.multiple_of(256 * ((z + n) % 8), 256)
        return wacc[pl.ds(2048 * k + at, 256), :] + wrecv0[pl.ds(at, 256), :].astype(F32)

    def w_ring():
        w0.wait_recv()

        def one(n):
            wsend1[n - 1] = two_cores(n).astype(BF16)
            w1_copy(n).start()

        each(1, 8, one)
        wsum[...] = two_cores(0)

    def w_plane():
        take(wrecv1, r_w.at[1])
        total = wsum[...]
        for n in range(7):
            total += wrecv1[n].astype(F32)
        wsum[...] = total
        wsend2[...] = wsum[...].astype(BF16).reshape(16, 16, 128)
        each(1, 16, lambda n: w2_copy(n).start())

    def w_ring_back():
        take(wrecv2, r_w.at[2])
        total = wsum[pl.ds(pl.multiple_of(16 * spot(0), 16), 16), :]
        for n in range(15):
            total += wrecv2[n].astype(F32)
        wsend3[...] = total.astype(BF16)
        wfull[k * 8 + z, spot(0)] = wsend3[...]
        each(1, 8, lambda n: w3_copy(n).start())

    def w_plane_back():
        take(wsend2.at[pl.ds(0, 7)], r_w.at[3])
        each(1, 16, lambda n: w4_copy(n).start())

    part5 = wfull.at[pl.ds(k * 8, 8)]
    w5 = remote(part5, part5, s_w.at[5], r_w.at[5], sibling)

    def pass_on(f):
        take(grads[f].at[pl.ds(0, 7), 0], r_g.at[f])
        gf_copy(f).start()
        gf_copy(f).wait_recv()

    def z_copy(f, d, s, p):
        part = pl.ds(0, 2) if s > 0 else pl.ds(d, 1)
        to = across[d] if s == 3 and p == 1 else ahead[d]
        return remote(
            zstage.at[f, d, s, p, part], zrecv.at[f, d, s, p, part],
            s_z.at[f], r_z.at[f, d, s, p], to)

    def x_copy(f):
        return remote(xstage.at[f], xrecv.at[f], s_z.at[f], r_y.at[f], partner)

    def term(f, p, zz, h):
        return scan[f, last_b[2 * (((xh + p) % 2) * 8 + zz % 8) + h]]

    def z_step(f, s):
        for p in (1, 0):
            for d in (0, 1):
                target = z + sign[d] * (4 - s)
                if s > 0:
                    z_copy(f, d, s - 1, p).wait_recv()
                for h in (0, 1):
                    if s == 0 and h != d:
                        continue
                    v = term(f, p, target, h)
                    if s > 1 or (s == 1 and h == d):
                        v = v + zrecv[f, d, s - 1, p, h].astype(F32)
                    zstage[f, d, s, p, h] = v.astype(BF16)
                z_copy(f, d, s, p).start()

    w_ring()
    for f in (0, 1):
        pass_on(f)
        aggregate(f, valt, rows, prev_b, lambda f, i: grads[f][i // 4, (i // 2) % 2, i % 2])
        z_step(f, 0)
        for h in (0, 1):
            xstage[f, h] = term(f, 1, z, h).astype(BF16)
        x_copy(f).start()
    w_plane()
    z_step(0, 1)
    z_step(1, 1)
    w_ring_back()
    z_step(0, 2)
    z_step(1, 2)
    w_plane_back()
    z_step(0, 3)
    z_step(1, 3)

    def arrive(f):
        x_copy(f).wait_recv()
        for p in (0, 1):
            for d in (0, 1):
                z_copy(f, d, 3, p).wait_recv()
        for h in (0, 1):
            v = term(f, 0, z, h) + xrecv[f, h].astype(F32)
            for p in (0, 1):
                for d in (0, 1):
                    v = v + zrecv[f, d, 3, p, h].astype(F32)
            gxs[f, h] = v.astype(BF16)
        stores.append(pltpu.make_async_copy(gxs.at[f], gx.at[:, :, halves[f]], sem_out.at[1 + f]))
        stores[-1].start()

    arrive(0)
    arrive(1)
    take(wfull.at[pl.ds(0, 8), pl.ds(0, 15)], r_w.at[4])
    w5.start()
    w5.wait_recv()
    for h in (0, 1):
        one = pltpu.make_async_copy(
            wfull.at[pl.ds(4 * h, 4)], gwout.at[:, :, :, halves[h]], sem_out.at[3])
        one.start()
    for t in range(8):
        one = pltpu.make_async_copy(
            wfull.at[8 + t], gwin.at[:, :, pl.ds(128 * t, 128)], sem_out.at[3])
        one.start()

    for one in stores:
        one.wait()
    take(wfull, sem_out.at[3])
    for f in (0, 1):
        take(feats[f].at[pl.ds(0, 30)], s_ag.at[f])
        take(feats[f].at[pl.ds(0, 30)], s_z.at[f])
        for g in (0, 1):
            p_copy(f, g).wait_send()
        take(qrecv.at[f], s_q.at[f])
        take(qrecv.at[f], s_g.at[f])
        gf_copy(f).wait_send()
    w0.wait_send()
    take(wrecv1, s_w.at[1])
    take(wrecv2, s_w.at[2])
    take(wsend2.at[pl.ds(0, 7)], s_w.at[3])
    take(wfull.at[pl.ds(0, 8), pl.ds(0, 15)], s_w.at[4])
    w5.wait_send()


def finish(*refs):
    inputs, outputs, here, wide, sem = refs[:4], refs[4:8], refs[8:12], refs[12:14], refs[14]
    halves = []
    for i in (2, 3, 0, 1):
        n = inputs[i].shape[0] // 2
        halves += [(i, pl.ds(n * h, n), h) for h in (0, 1)]
    ins = [
        pltpu.make_async_copy(inputs[i].at[at], here[i].at[at], sem.at[i, h]) for i, at, h in halves
    ]
    for one in ins:
        one.start()
    outs = []
    for (i, at, h), one in zip(halves, ins):
        one.wait()
        source = here[i] if i < 2 else wide[i - 2]
        if i >= 2:
            source[at] = here[i][at].astype(F32)
        outs.append(pltpu.make_async_copy(source.at[at], outputs[i].at[at], sem.at[i + 4, h]))
        outs[-1].start()
    for one in outs:
        one.wait()


def body(features, block_values, block_rows, block_cols, block_count, weight_in, weight_out, cot):
    vm = lambda *shape, t=BF16: pltpu.VMEM(shape, t)
    dma = lambda *shape: pltpu.SemaphoreType.DMA(shape)
    hbm = pl.BlockSpec(memory_space=pltpu.HBM)
    sm = lambda *shape: pltpu.SMEM(shape, jnp.int32)
    lout, gx, gwin, gwout = pl.pallas_call(
        kernel,
        out_shape=(
            jax.ShapeDtypeStruct((2 * BLK, WIDTH), BF16),
            jax.ShapeDtypeStruct((2, BLK, WIDTH), BF16),
            jax.ShapeDtypeStruct((16, 16, HID), BF16),
            jax.ShapeDtypeStruct((4, 16, 16, WIDTH), BF16),
        ),
        in_specs=[hbm] * 8,
        out_specs=(hbm,) * 4,
        scratch_shapes=[
            sm(1, 1, SLOTS), sm(1, 1, SLOTS), sm(1, 1), sm(SLOTS), sm(SLOTS), sm(SLOTS), sm(SLOTS),
            vm(SLOTS, BLK, BLK), vm(SLOTS, BLK, BLK), vm(WIDTH, HID), vm(HID, WIDTH),
            vm(2 * BLK, WIDTH), vm(2 * BLK, WIDTH), vm(2, 2, BLK, HALF),
            vm(BLOCKS, BLK, HALF), vm(BLOCKS, BLK, HALF),
            vm(8, 2, 2, BLK, HALF), vm(8, 2, 2, BLK, HALF),
            vm(2, SLOTS + 1, BLK, HALF, t=F32),
            vm(2, 8, 2, BLK, HALF), vm(2, 8, 2, BLK, HALF), vm(2, 7, 2, BLK, HALF),
            vm(2, 7, 2, BLK, HALF), vm(2, 2, BLK, HALF, t=F32),
            vm(2, 2, 4, 2, 2, BLK, HALF), vm(2, 2, 4, 2, 2, BLK, HALF),
            vm(2, 2, BLK, HALF), vm(2, 2, BLK, HALF), vm(2, 2, BLK, HALF),
            vm(4096, 128, t=F32), vm(2048, 128), vm(2048, 128), vm(7, 256, 128),
            vm(7, 256, 128), vm(256, 128, t=F32), vm(16, 16, 128), vm(15, 16, 128),
            vm(16, 128), vm(16, 16, 16, 128),
            dma(9), dma(4), dma(2), dma(2, 2, 4, 2), dma(2), dma(2),
            dma(2, 2), dma(2, 2), dma(2), dma(2), dma(2), dma(2), dma(2), dma(2),
            dma(2), dma(2, 2, 4, 2), dma(6), dma(6),
        ],
        compiler_params=pltpu.CompilerParams(
            collective_id=0, has_side_effects=True, vmem_limit_bytes=60 * 2**20
        ),
        name="layer",
    )(
        block_rows, block_cols, block_count, features.reshape(2, BLK, WIDTH),
        block_values[0, 0], weight_in, weight_out, cot,
    )
    lout, gx, gwin, gwout = pl.pallas_call(
        finish,
        out_shape=(
            jax.ShapeDtypeStruct((2 * BLK, WIDTH), BF16),
            jax.ShapeDtypeStruct((2, BLK, WIDTH), BF16),
            jax.ShapeDtypeStruct((WIDTH, HID), F32),
            jax.ShapeDtypeStruct((HID, WIDTH), F32),
        ),
        in_specs=[hbm] * 4,
        out_specs=(hbm,) * 4,
        scratch_shapes=[
            vm(2 * BLK, WIDTH), vm(2, BLK, WIDTH), vm(WIDTH, HID), vm(HID, WIDTH),
            vm(WIDTH, HID, t=F32), vm(HID, WIDTH, t=F32), dma(8, 2),
        ],
        compiler_params=pltpu.CompilerParams(vmem_limit_bytes=60 * 2**20),
        name="finish",
    )(lout, gx, gwin.reshape(WIDTH, HID), gwout.reshape(HID, WIDTH))
    return lout, gx.reshape(2 * BLK, WIDTH), gwin, gwout


def solution(mesh):
    return jax.shard_map(
        body,
        mesh=mesh,
        in_specs=(
            P(("col", "row"), None),
            P("row", "col", None, None, None),
            P("row", "col", None),
            P("row", "col", None),
            P("row", "col"),
            P(),
            P(),
            P(("row", "col"), None),
        ),
        out_specs=(P(("row", "col"), None), P(("col", "row"), None), P(), P()),
        check_vma=False,
    )
```

```python
import jax
import jax.numpy as jnp
from jax import lax
from jax.experimental import pallas as pl
from jax.experimental.pallas import tpu as pltpu
from jax.sharding import PartitionSpec as P

MESH = pl.DeviceIdType.MESH
F32, BF16 = jnp.float32, jnp.bfloat16
BLK, HALF, WIDTH, HID, SLOTS, BLOCKS = 128, 128, 256, 1024, 32, 32


def dot(a, b, ca=1, cb=0):
    return lax.dot_general(a, b, (((ca,), (cb,)), ((), ())), preferred_element_type=F32)


def kernel(
    rows_h, cols_h, count_h, feat_h, values_h, win_h, wout_h, cot_h,
    lout, gx, gwin, gwout,
    rows, cols, count, prev_f, prev_b, last_f, last_b,
    val, valt, win, wout, cot, louts, gxs,
    feats0, feats1, grads0, grads1, scan, pstage, precv, qstage, qrecv, own,
    zstage, zrecv, xstage, xrecv, gpool,
    gact, acts, gpres, pools, wacc, wstage, wrecv0, wsend1, wrecv1, wsum, wsend2, wrecv2, wsend3, wfull,
    sem_in, sem_out, s_ag, r_ag, r_x, r_y, s_p, r_p, s_q, r_q, s_g, r_g, s_gf, r_gf,
    s_z, r_z, s_w, r_w,
):
    feats, grads = (feats0, feats1), (grads0, grads1)
    r, c = lax.axis_index("row"), lax.axis_index("col")
    xh, z = r // 8, r % 8
    j, k = c // 2, c % 2
    xl, y = j // 4, j % 4
    sibling = (r, 2 * j + 1 - k)

    def chip(m):
        return ((xl + m // 4) % 2) * 4 + (y + m % 4) % 4

    def behind(m):
        return ((xl + m // 4) % 2) * 4 + (y + 4 - m % 4) % 4

    def along(n):
        return (xh * 8 + (z + n) % 8, c)

    x = 2 * xh + xl

    def spot(n):
        return ((x + n // 4) % 4) * 4 + (y + n % 4) % 4

    def level(q):
        return ((q // 8) * 8 + z, ((q // 4) % 2) * 8 + (q % 4) * 2 + k)

    partner = ((1 - xh) * 8 + z, c)
    sign = (1, 7)
    ahead = [(xh * 8 + (z + g) % 8, c) for g in sign]
    across = [((1 - xh) * 8 + (z + g) % 8, c) for g in sign]

    def remote(src, dst, ss, rs, to):
        return pltpu.make_async_remote_copy(
            src_ref=src, dst_ref=dst, send_sem=ss, recv_sem=rs, device_id=to, device_id_type=MESH
        )

    def take(view, sem):
        pltpu.make_async_copy(view, view, sem).wait()

    def each(lo, hi, f):
        lax.fori_loop(lo, hi, lambda i, _: (f(i), 0)[1], 0)

    halves = [pl.ds(0, HALF), pl.ds(HALF, HALF)]
    pairs = [(feat_h.at[:, :, halves[f]], feats[f].at[pl.ds(2 * r, 2)]) for f in (0, 1)]
    pairs += [(count_h, count), (rows_h, rows), (cols_h, cols), (values_h, val)]
    pairs += [(win_h, win), (wout_h, wout), (cot_h, cot)]
    loads = [pltpu.make_async_copy(a, b, sem_in.at[i]) for i, (a, b) in enumerate(pairs)]
    for one in loads[:5]:
        one.start()

    barrier = pltpu.get_barrier_semaphore()

    def greet(to):
        pl.semaphore_signal(barrier, inc=1, device_id=to, device_id_type=MESH)

    greet(sibling)
    each(1, 16, lambda n: greet(level(spot(n))))
    each(1, 8, lambda n: greet(along(n)))
    for one in across:
        greet(one)
    pl.semaphore_wait(barrier, 25)

    def ag_copy(f, d, s, p):
        plane = (xh + (p if s > 0 else 0)) % 2
        at = 2 * (plane * 8 + (z + (8 - sign[d]) * s) % 8)
        part = feats[f].at[pl.ds(at, 2) if s < 3 else pl.ds(at + d, 1)]
        to = across[d] if s == 0 and p == 1 else ahead[d]
        return remote(part, part, s_ag.at[f], r_ag.at[f, d, s, p], to)

    def swap(f):
        part = feats[f].at[pl.ds(2 * r, 2)]
        return remote(part, part, s_ag.at[f], r_x.at[f], partner)

    for f in (0, 1):
        loads[f].wait()
        for p in (0, 1):
            for d in (0, 1):
                ag_copy(f, d, 0, p).start()

    for one in loads[5:]:
        one.start()
    for one in loads[2:6]:
        one.wait()

    def mask(s):
        live = jnp.where(s < count[0, 0], 1.0, 0.0).astype(F32)
        masked = val[s].astype(F32) * live
        val[s] = masked.astype(BF16)
        valt[s] = masked.T.astype(BF16)

    def lists(s):
        for keys, prev, last in ((rows, prev_f, last_f), (cols, prev_b, last_b)):
            mine = keys[0, 0, s]
            before, newest = jnp.int32(0), jnp.int32(0)
            for t in range(SLOTS):
                before = jnp.where((keys[0, 0, t] == mine) & (t < s), t + 1, before)
                newest = jnp.where(keys[0, 0, t] == s, t + 1, newest)
            prev[s] = before
            last[s] = newest

    def pass_features(f, s, p):
        for d in (0, 1):
            ag_copy(f, d, s - 1, p).wait_recv()
            ag_copy(f, d, s, p).start()

    each(0, 16, mask)
    pass_features(0, 1, 0)
    pass_features(1, 1, 0)
    each(16, 32, mask)
    pass_features(0, 1, 1)
    for f in (0, 1):
        swap(f).start()
    pass_features(0, 2, 0)
    pass_features(1, 1, 1)
    pass_features(1, 2, 0)
    each(0, 12, lists)
    pass_features(0, 2, 1)
    pass_features(0, 3, 0)
    each(12, 24, lists)
    pass_features(1, 2, 1)
    pass_features(1, 3, 0)
    each(24, 32, lists)
    pass_features(0, 3, 1)
    for one in loads[6:]:
        one.wait()
    for t in range(4):
        gact[t] = dot(cot[...], wout[pl.ds(t * 256, 256), :], 1, 1)
    pass_features(1, 3, 1)

    def ag_wait(f):
        swap(f).wait_recv()
        for d in (0, 1):
            for p in (0, 1):
                ag_copy(f, d, 3, p).wait_recv()

    def aggregate(f, vals, source, prev, block):
        scan[f, 0] = jnp.zeros((BLK, HALF), F32)

        def some(g):
            for u in range(8):
                s = g * 8 + u
                scan[f, s + 1] = dot(vals[s], block(f, source[0, 0, s])) + scan[f, prev[s]]

        each(0, SLOTS // 8, some)

    def p_copy(f, g):
        part = pl.ds(4 * g, 4)
        return remote(
            pstage.at[f, part], precv.at[f, part], s_p.at[f, g], r_p.at[f, g], sibling)

    def q_copy(f, h, m):
        return remote(
            qstage.at[f, h, m - 1], qrecv.at[f, h, m - 1], s_q.at[f], r_q.at[f, h],
            (r, 2 * chip(m) + k))

    def give(f):
        for g in (0, 1):
            def one(i):
                at = 2 * (2 * chip((i + 1) % 8) + 1 - k)
                for h in (0, 1):
                    pstage[f, i, h] = scan[f, last_f[at + h]].astype(BF16)

            each(4 * g, 4 * g + 4, one)
            p_copy(f, g).start()

    def spread(f):
        def pair_sum(i, h):
            mine = scan[f, last_f[2 * (2 * chip((i + 1) % 8) + k) + h]]
            return mine + precv[f, i, h].astype(F32)

        for h in (0, 1):
            def one(i):
                qstage[f, h, i] = pair_sum(i, h).astype(BF16)
                q_copy(f, h, i + 1).start()

            if h == 0:
                p_copy(f, 0).wait_recv()
            each(0, 4, one)
            if h == 0:
                p_copy(f, 1).wait_recv()
            each(4, 7, one)
        for h in (0, 1):
            own[f, h] = pair_sum(7, h)

    def collect(f, h):
        take(qrecv.at[f, h], r_q.at[f, h])
        total = own[f, h]
        for m in range(7):
            total += qrecv[f, h, m].astype(F32)
        return total

    for f in (0, 1):
        ag_wait(f)
        aggregate(f, val, cols, prev_f, lambda f, i: feats[f][i])
        give(f)
        spread(f)
    def g_copy(f, h, m):
        return remote(
            gpool.at[f, h], grads[f].at[j, k, h], s_g.at[f], r_g.at[f], (r, 2 * chip(m) + k))

    def gf_copy(f):
        part = grads[f].at[:, k]
        return remote(part, part, s_gf.at[f], r_gf.at[f], sibling)

    a0, a1 = 0.7978845608028654, 0.044715
    for h in (0, 1):
        block = pl.ds(h * BLK, BLK)
        some = jnp.concatenate([collect(f, h).astype(BF16) for f in (0, 1)], axis=1)
        pools[block, :] = some
        back = cot[block, :].astype(F32)
        for t in range(4):
            w_in = win[:, pl.ds(t * 256, 256)]
            pre = dot(some, w_in)
            square = pre * pre
            th = jnp.tanh(a0 * (pre + a1 * (square * pre)))
            cdf = 0.5 * (1.0 + th)
            acts[t, block, :] = (pre * cdf).astype(BF16)
            slope = cdf + 0.5 * pre * (1.0 - th * th) * (a0 * (1.0 + 3.0 * a1 * square))
            gpre = (gact[t, block, :] * slope).astype(BF16)
            gpres[t, block, :] = gpre
            back = back + dot(gpre, w_in, 1, 1)
        for f in (0, 1):
            gpool[f, h] = back[:, f * HALF:(f + 1) * HALF].astype(BF16)
        if h == 0:
            each(1, 8, lambda m: g_copy(0, 0, m).start())
    for f, h in ((0, 1), (1, 0), (1, 1)):
        each(1, 8, lambda m: g_copy(f, h, m).start())
    for f in (0, 1):
        grads[f][j, k] = gpool[f]

    ct, pooled = cot[...], pools[...]
    out = pooled.astype(F32)
    for t in range(4):
        g_out = dot(acts[t], ct, 0, 0)
        g_in = dot(pooled, gpres[t], 0, 0)
        for h in (0, 1):
            wacc[pl.ds(h * 1024 + t * 256, 256), :] = g_out[:, h * 128:(h + 1) * 128]
            wacc[pl.ds(2048 + (2 * t + h) * 256, 256), :] = g_in[:, h * 128:(h + 1) * 128]

    wstage[...] = wacc[pl.ds(2048 * (1 - k), 2048), :].astype(BF16)
    w0 = remote(wstage, wrecv0, s_w.at[0], r_w.at[0], sibling)
    w0.start()
    for t in range(4):
        out = out + dot(acts[t], wout[pl.ds(t * 256, 256), :])
    louts[...] = out.astype(BF16)
    stores = [pltpu.make_async_copy(louts, lout, sem_out.at[0])]
    stores[0].start()

    def w1_copy(n):
        return remote(
            wsend1.at[n - 1], wrecv1.at[n - 1], s_w.at[1], r_w.at[1], level(spot(n)))

    def w2_copy(n):
        return remote(
            wsend2.at[(z + n) % 8], wrecv2.at[n - 1], s_w.at[2], r_w.at[2], along(n))

    def w3_copy(n):
        return remote(wsend3, wfull.at[k, spot(0), z], s_w.at[3], r_w.at[3], along(n))

    def w4_copy(n):
        part = wfull.at[k, spot(0)]
        return remote(part, part, s_w.at[4], r_w.at[4], level(spot(n)))

    def two_cores(n):
        at = pl.multiple_of(128 * spot(n), 128)
        return wacc[pl.ds(2048 * k + at, 128), :] + wrecv0[pl.ds(at, 128), :].astype(F32)

    def w_plane():
        w0.wait_recv()

        def one(n):
            wsend1[n - 1] = two_cores(n).astype(BF16)
            w1_copy(n).start()

        each(1, 16, one)
        wsum[...] = two_cores(0)

    def w_ring():
        take(wrecv1, r_w.at[1])
        total = wsum[...]
        for n in range(15):
            total += wrecv1[n].astype(F32)
        wsum[...] = total
        wsend2[...] = total.astype(BF16).reshape(8, 16, 128)
        each(1, 8, lambda n: w2_copy(n).start())

    def w_ring_back():
        take(wrecv2, r_w.at[2])
        total = wsum[pl.ds(pl.multiple_of(16 * z, 16), 16), :]
        for n in range(7):
            total += wrecv2[n].astype(F32)
        wsend3[...] = total.astype(BF16)
        wfull[k, spot(0), z] = wsend3[...]
        each(1, 8, lambda n: w3_copy(n).start())

    def w_plane_back():
        take(wrecv2, r_w.at[3])
        each(1, 16, lambda n: w4_copy(n).start())

    part5 = wfull.at[k]
    w5 = remote(part5, part5, s_w.at[5], r_w.at[5], sibling)

    def pass_on(f):
        take(grads[f].at[pl.ds(0, 7), 0], r_g.at[f])
        gf_copy(f).start()

    def z_copy(f, d, s, p):
        part = pl.ds(0, 2) if s > 0 else pl.ds(d, 1)
        to = across[d] if s == 3 and p == 1 else ahead[d]
        return remote(
            zstage.at[f, d, s, p, part], zrecv.at[f, d, s, p, part],
            s_z.at[f], r_z.at[f, d, s, p], to)

    def x_copy(f):
        return remote(xstage.at[f], xrecv.at[f], s_z.at[f], r_y.at[f], partner)

    def term(f, p, zz, h):
        return scan[f, last_b[2 * (((xh + p) % 2) * 8 + zz % 8) + h]]

    def z_step(f, s):
        for p in (1, 0):
            for d in (0, 1):
                target = z + sign[d] * (4 - s)
                if s > 0:
                    z_copy(f, d, s - 1, p).wait_recv()
                for h in (0, 1):
                    if s == 0 and h != d:
                        continue
                    v = term(f, p, target, h)
                    if s > 1 or (s == 1 and h == d):
                        v = v + zrecv[f, d, s - 1, p, h].astype(F32)
                    zstage[f, d, s, p, h] = v.astype(BF16)
                z_copy(f, d, s, p).start()

    def back_product(f):
        gf_copy(f).wait_recv()
        aggregate(f, valt, rows, prev_b, lambda f, i: grads[f][i // 4, (i // 2) % 2, i % 2])
        z_step(f, 0)
        for h in (0, 1):
            xstage[f, h] = term(f, 1, z, h).astype(BF16)
        x_copy(f).start()

    w_plane()
    pass_on(0)
    back_product(0)
    z_step(0, 1)
    w_ring()
    pass_on(1)
    back_product(1)
    w_ring_back()
    z_step(0, 2)
    z_step(1, 1)
    w_plane_back()
    z_step(0, 3)
    z_step(1, 2)
    z_step(1, 3)

    def arrive(f):
        x_copy(f).wait_recv()
        for p in (0, 1):
            for d in (0, 1):
                z_copy(f, d, 3, p).wait_recv()
        for h in (0, 1):
            v = term(f, 0, z, h) + xrecv[f, h].astype(F32)
            for p in (0, 1):
                for d in (0, 1):
                    v = v + zrecv[f, d, 3, p, h].astype(F32)
            gxs[f, h] = v.astype(BF16)
        stores.append(pltpu.make_async_copy(gxs.at[f], gx.at[:, :, halves[f]], sem_out.at[1 + f]))
        stores[-1].start()

    arrive(0)
    take(wfull.at[k, pl.ds(0, 15)], r_w.at[4])
    w5.start()
    arrive(1)
    w5.wait_recv()
    for h in (0, 1):
        one = pltpu.make_async_copy(
            wfull.at[0, pl.ds(8 * h, 8)], gwout.at[:, :, :, halves[h]], sem_out.at[3])
        one.start()
    for t in range(8):
        one = pltpu.make_async_copy(
            wfull.at[1, pl.ds(2 * t, 2)], gwin.at[:, :, :, pl.ds(128 * t, 128)], sem_out.at[3])
        one.start()

    for one in stores:
        one.wait()
    take(wfull, sem_out.at[3])
    for f in (0, 1):
        take(feats[f].at[pl.ds(0, 30)], s_ag.at[f])
        take(feats[f].at[pl.ds(0, 30)], s_z.at[f])
        for g in (0, 1):
            p_copy(f, g).wait_send()
        take(qrecv.at[f], s_q.at[f])
        take(qrecv.at[f], s_g.at[f])
        gf_copy(f).wait_send()
    w0.wait_send()
    take(wrecv1, s_w.at[1])
    take(wrecv2, s_w.at[2])
    take(wrecv2, s_w.at[3])
    take(wfull.at[k, pl.ds(0, 15)], s_w.at[4])
    w5.wait_send()


def finish(*refs):
    inputs, outputs, here, wide, sem = refs[:4], refs[4:8], refs[8:12], refs[12:14], refs[14]
    halves = []
    for i in (2, 3, 0, 1):
        n = inputs[i].shape[0] // 2
        halves += [(i, pl.ds(n * h, n), h) for h in (0, 1)]
    ins = [
        pltpu.make_async_copy(inputs[i].at[at], here[i].at[at], sem.at[i, h]) for i, at, h in halves
    ]
    for one in ins:
        one.start()
    outs = []
    for (i, at, h), one in zip(halves, ins):
        one.wait()
        source = here[i] if i < 2 else wide[i - 2]
        if i >= 2:
            source[at] = here[i][at].astype(F32)
        outs.append(pltpu.make_async_copy(source.at[at], outputs[i].at[at], sem.at[i + 4, h]))
        outs[-1].start()
    for one in outs:
        one.wait()


def body(features, block_values, block_rows, block_cols, block_count, weight_in, weight_out, cot):
    vm = lambda *shape, t=BF16: pltpu.VMEM(shape, t)
    dma = lambda *shape: pltpu.SemaphoreType.DMA(shape)
    hbm = pl.BlockSpec(memory_space=pltpu.HBM)
    sm = lambda *shape: pltpu.SMEM(shape, jnp.int32)
    lout, gx, gwin, gwout = pl.pallas_call(
        kernel,
        out_shape=(
            jax.ShapeDtypeStruct((2 * BLK, WIDTH), BF16),
            jax.ShapeDtypeStruct((2, BLK, WIDTH), BF16),
            jax.ShapeDtypeStruct((2, 8, 16, HID), BF16),
            jax.ShapeDtypeStruct((8, 8, 16, WIDTH), BF16),
        ),
        in_specs=[hbm] * 8,
        out_specs=(hbm,) * 4,
        scratch_shapes=[
            sm(1, 1, SLOTS), sm(1, 1, SLOTS), sm(1, 1), sm(SLOTS), sm(SLOTS), sm(SLOTS), sm(SLOTS),
            vm(SLOTS, BLK, BLK), vm(SLOTS, BLK, BLK), vm(WIDTH, HID), vm(HID, WIDTH),
            vm(2 * BLK, WIDTH), vm(2 * BLK, WIDTH), vm(2, 2, BLK, HALF),
            vm(BLOCKS, BLK, HALF), vm(BLOCKS, BLK, HALF),
            vm(8, 2, 2, BLK, HALF), vm(8, 2, 2, BLK, HALF),
            vm(2, SLOTS + 1, BLK, HALF, t=F32),
            vm(2, 8, 2, BLK, HALF), vm(2, 8, 2, BLK, HALF), vm(2, 2, 7, BLK, HALF),
            vm(2, 2, 7, BLK, HALF), vm(2, 2, BLK, HALF, t=F32),
            vm(2, 2, 4, 2, 2, BLK, HALF), vm(2, 2, 4, 2, 2, BLK, HALF),
            vm(2, 2, BLK, HALF), vm(2, 2, BLK, HALF), vm(2, 2, BLK, HALF),
            vm(4, 256, 256, t=F32), vm(4, 256, 256), vm(4, 256, 256), vm(2 * BLK, WIDTH),
            vm(4096, 128, t=F32), vm(2048, 128), vm(2048, 128), vm(15, 128, 128),
            vm(15, 128, 128), vm(128, 128, t=F32), vm(8, 16, 128), vm(7, 16, 128),
            vm(16, 128), vm(2, 16, 8, 16, 128),
            dma(9), dma(4), dma(2), dma(2, 2, 4, 2), dma(2), dma(2),
            dma(2, 2), dma(2, 2), dma(2), dma(2, 2), dma(2), dma(2), dma(2), dma(2),
            dma(2), dma(2, 2, 4, 2), dma(6), dma(6),
        ],
        compiler_params=pltpu.CompilerParams(
            collective_id=0, has_side_effects=True, vmem_limit_bytes=60 * 2**20
        ),
        name="layer",
    )(
        block_rows, block_cols, block_count, features.reshape(2, BLK, WIDTH),
        block_values[0, 0], weight_in, weight_out, cot,
    )
    lout, gx, gwin, gwout = pl.pallas_call(
        finish,
        out_shape=(
            jax.ShapeDtypeStruct((2 * BLK, WIDTH), BF16),
            jax.ShapeDtypeStruct((2, BLK, WIDTH), BF16),
            jax.ShapeDtypeStruct((WIDTH, HID), F32),
            jax.ShapeDtypeStruct((HID, WIDTH), F32),
        ),
        in_specs=[hbm] * 4,
        out_specs=(hbm,) * 4,
        scratch_shapes=[
            vm(2 * BLK, WIDTH), vm(2, BLK, WIDTH), vm(WIDTH, HID), vm(HID, WIDTH),
            vm(WIDTH, HID, t=F32), vm(HID, WIDTH, t=F32), dma(8, 2),
        ],
        compiler_params=pltpu.CompilerParams(vmem_limit_bytes=60 * 2**20),
        name="finish",
    )(lout, gx, gwin.reshape(WIDTH, HID), gwout.reshape(HID, WIDTH))
    return lout, gx.reshape(2 * BLK, WIDTH), gwin, gwout


def solution(mesh):
    return jax.shard_map(
        body,
        mesh=mesh,
        in_specs=(
            P(("col", "row"), None),
            P("row", "col", None, None, None),
            P("row", "col", None),
            P("row", "col", None),
            P("row", "col"),
            P(),
            P(),
            P(("row", "col"), None),
        ),
        out_specs=(P(("row", "col"), None), P(("col", "row"), None), P(), P()),
        check_vma=False,
    )
```

```python
import jax
import jax.numpy as jnp
from jax import lax
from jax.experimental import pallas as pl
from jax.experimental.pallas import tpu as pltpu
from jax.sharding import PartitionSpec as P

MESH = pl.DeviceIdType.MESH
F32, BF16 = jnp.float32, jnp.bfloat16
BLK, HALF, WIDTH, HID, SLOTS, BLOCKS = 128, 128, 256, 1024, 32, 32


def dot(a, b, ca=1, cb=0):
    return lax.dot_general(a, b, (((ca,), (cb,)), ((), ())), preferred_element_type=F32)


def kernel(
    rows_h, cols_h, count_h, feat_h, values_h, win_h, wout_h, cot_h,
    lout, gx, gwin, gwout,
    rows, cols, count, prev_f, prev_b, last_f, last_b,
    val, valt, win, wout, cot, louts, gxs,
    feats0, feats1, grads0, grads1, scan, pstage, precv, qstage, qrecv, own,
    zstage, zrecv, xstage, xrecv, gpool,
    gact, acts, gpres, pools, wacc, wstage, wrecv0, wsend1, wrecv1, wsum, wsend2, wrecv2, wsend3, wfull,
    sem_in, sem_out, s_ag, r_ag, r_x, r_y, s_p, r_p, s_q, r_q, s_g, r_g, s_gf, r_gf,
    s_z, r_z, s_w, r_w,
):
    feats, grads = (feats0, feats1), (grads0, grads1)
    r, c = lax.axis_index("row"), lax.axis_index("col")
    xh, z = r // 8, r % 8
    j, k = c // 2, c % 2
    xl, y = j // 4, j % 4
    sibling = (r, 2 * j + 1 - k)

    def chip(m):
        return ((xl + m // 4) % 2) * 4 + (y + m % 4) % 4

    def behind(m):
        return ((xl + m // 4) % 2) * 4 + (y + 4 - m % 4) % 4

    def along(n):
        return (xh * 8 + (z + n) % 8, c)

    x = 2 * xh + xl

    def spot(n):
        return ((x + n // 4) % 4) * 4 + (y + n % 4) % 4

    def level(q):
        return ((q // 8) * 8 + z, ((q // 4) % 2) * 8 + (q % 4) * 2 + k)

    partner = ((1 - xh) * 8 + z, c)
    sign = (1, 7)
    ahead = [(xh * 8 + (z + g) % 8, c) for g in sign]
    far = [(xh * 8 + (z + 2 * g) % 8, c) for g in sign]
    across = [((1 - xh) * 8 + (z + g) % 8, c) for g in sign]

    def remote(src, dst, ss, rs, to):
        return pltpu.make_async_remote_copy(
            src_ref=src, dst_ref=dst, send_sem=ss, recv_sem=rs, device_id=to, device_id_type=MESH
        )

    def take(view, sem):
        pltpu.make_async_copy(view, view, sem).wait()

    def each(lo, hi, f):
        lax.fori_loop(lo, hi, lambda i, _: (f(i), 0)[1], 0)

    halves = [pl.ds(0, HALF), pl.ds(HALF, HALF)]
    pairs = [(feat_h.at[:, :, halves[f]], feats[f].at[pl.ds(2 * r, 2)]) for f in (0, 1)]
    pairs += [(count_h, count), (rows_h, rows), (cols_h, cols), (values_h, val)]
    pairs += [(win_h, win), (wout_h, wout), (cot_h, cot)]
    loads = [pltpu.make_async_copy(a, b, sem_in.at[i]) for i, (a, b) in enumerate(pairs)]
    for one in loads[:5]:
        one.start()

    barrier = pltpu.get_barrier_semaphore()

    def greet(to):
        pl.semaphore_signal(barrier, inc=1, device_id=to, device_id_type=MESH)

    greet(sibling)
    each(1, 16, lambda n: greet(level(spot(n))))
    each(1, 8, lambda n: greet(along(n)))
    for one in across:
        greet(one)
    pl.semaphore_wait(barrier, 25)

    def ag_copy(f, d, s, p):
        plane = (xh + (p if 0 < s < 3 else 0)) % 2
        away = s if s < 3 else 4 if p == 1 else 2
        at = 2 * (plane * 8 + (z + (8 - sign[d]) * away) % 8)
        part = feats[f].at[pl.ds(at, 2) if s < 3 else pl.ds(at + d, 1)]
        to = ahead[d]
        if p == 1 and s == 0:
            to = across[d]
        if s == 3:
            to = partner if p == 1 else far[d]
        return remote(part, part, s_ag.at[f], r_ag.at[f, d, s, p], to)

    def swap(f):
        part = feats[f].at[pl.ds(2 * r, 2)]
        return remote(part, part, s_ag.at[f], r_x.at[f], partner)

    def send_features(f, p):
        for d in (0, 1):
            ag_copy(f, d, 0, p).start()

    loads[0].wait()
    send_features(0, 0)
    send_features(0, 1)
    loads[1].wait()
    send_features(1, 0)
    for one in loads[5:]:
        one.start()
    for one in loads[2:6]:
        one.wait()

    def mask(s):
        live = jnp.where(s < count[0, 0], 1.0, 0.0).astype(F32)
        masked = val[s].astype(F32) * live
        val[s] = masked.astype(BF16)
        valt[s] = masked.T.astype(BF16)

    def lists(s):
        for keys, prev, last in ((rows, prev_f, last_f), (cols, prev_b, last_b)):
            mine = keys[0, 0, s]
            before, newest = jnp.int32(0), jnp.int32(0)
            for t in range(SLOTS):
                before = jnp.where((keys[0, 0, t] == mine) & (t < s), t + 1, before)
                newest = jnp.where(keys[0, 0, t] == s, t + 1, newest)
            prev[s] = before
            last[s] = newest

    def pass_features(f, s, p):
        for d in (0, 1):
            ag_copy(f, d, s - 1, p).wait_recv()
            if s == 2 and p == 0:
                ag_copy(f, d, 3, 0).start()
            ag_copy(f, d, s, p).start()

    def pass_last(f):
        for d in (0, 1):
            ag_copy(f, d, 3, 0).wait_recv()
            ag_copy(f, d, 3, 1).start()

    each(0, 8, mask)
    pass_features(0, 1, 0)
    send_features(1, 1)
    each(8, 16, mask)
    pass_features(0, 1, 1)
    pass_features(1, 1, 0)
    swap(0).start()
    each(16, 24, mask)
    pass_features(0, 2, 0)
    pass_features(1, 1, 1)
    swap(1).start()
    each(24, 32, mask)
    pass_features(0, 2, 1)
    pass_features(1, 2, 0)
    each(0, 16, lists)
    pass_last(0)
    each(16, 32, lists)
    pass_features(1, 2, 1)
    for one in loads[6:]:
        one.wait()
    for t in range(4):
        gact[t] = dot(cot[...], wout[pl.ds(t * 256, 256), :], 1, 1)
    pass_last(1)

    def ag_wait(f):
        swap(f).wait_recv()
        for d in (0, 1):
            for p in (0, 1):
                ag_copy(f, d, 2, p).wait_recv()
            ag_copy(f, d, 3, 1).wait_recv()

    def aggregate(f, vals, source, prev, block):
        scan[f, 0] = jnp.zeros((BLK, HALF), F32)

        def some(g):
            for u in range(8):
                s = g * 8 + u
                scan[f, s + 1] = dot(vals[s], block(f, source[0, 0, s])) + scan[f, prev[s]]

        each(0, SLOTS // 8, some)

    def p_copy(f, g):
        part = pl.ds(4 * g, 4)
        return remote(
            pstage.at[f, part], precv.at[f, part], s_p.at[f, g], r_p.at[f, g], sibling)

    def q_copy(f, h, m):
        return remote(
            qstage.at[f, h, m - 1], qrecv.at[f, h, m - 1], s_q.at[f], r_q.at[f, h],
            (r, 2 * chip(m) + k))

    def give(f):
        for g in (0, 1):
            def one(i):
                at = 2 * (2 * chip((i + 1) % 8) + 1 - k)
                for h in (0, 1):
                    pstage[f, i, h] = scan[f, last_f[at + h]].astype(BF16)

            each(4 * g, 4 * g + 4, one)
            p_copy(f, g).start()

    def spread(f):
        def pair_sum(i, h):
            mine = scan[f, last_f[2 * (2 * chip((i + 1) % 8) + k) + h]]
            return mine + precv[f, i, h].astype(F32)

        for h in (0, 1):
            def one(i):
                qstage[f, h, i] = pair_sum(i, h).astype(BF16)
                q_copy(f, h, i + 1).start()

            if h == 0:
                p_copy(f, 0).wait_recv()
            each(0, 4, one)
            if h == 0:
                p_copy(f, 1).wait_recv()
            each(4, 7, one)
        for h in (0, 1):
            own[f, h] = pair_sum(7, h)

    def collect(f, h):
        take(qrecv.at[f, h], r_q.at[f, h])
        total = own[f, h]
        for m in range(7):
            total += qrecv[f, h, m].astype(F32)
        return total

    for f in (0, 1):
        ag_wait(f)
        aggregate(f, val, cols, prev_f, lambda f, i: feats[f][i])
        give(f)
        spread(f)
    def g_copy(f, h, m):
        return remote(
            gpool.at[f, h], grads[f].at[j, k, h], s_g.at[f], r_g.at[f], (r, 2 * chip(m) + k))

    def gf_copy(f):
        part = grads[f].at[:, k]
        return remote(part, part, s_gf.at[f], r_gf.at[f], sibling)

    a0, a1 = 0.7978845608028654, 0.044715
    for h in (0, 1):
        block = pl.ds(h * BLK, BLK)
        some = jnp.concatenate([collect(f, h).astype(BF16) for f in (0, 1)], axis=1)
        pools[block, :] = some
        back = cot[block, :].astype(F32)
        for t in range(4):
            w_in = win[:, pl.ds(t * 256, 256)]
            pre = dot(some, w_in)
            square = pre * pre
            th = jnp.tanh(a0 * (pre + a1 * (square * pre)))
            cdf = 0.5 * (1.0 + th)
            acts[t, block, :] = (pre * cdf).astype(BF16)
            slope = cdf + 0.5 * pre * (1.0 - th * th) * (a0 * (1.0 + 3.0 * a1 * square))
            gpre = (gact[t, block, :] * slope).astype(BF16)
            gpres[t, block, :] = gpre
            back = back + dot(gpre, w_in, 1, 1)
        for f in (0, 1):
            gpool[f, h] = back[:, f * HALF:(f + 1) * HALF].astype(BF16)
        if h == 0:
            each(1, 8, lambda m: g_copy(0, 0, m).start())
    for f, h in ((0, 1), (1, 0), (1, 1)):
        each(1, 8, lambda m: g_copy(f, h, m).start())
    for f in (0, 1):
        grads[f][j, k] = gpool[f]

    ct, pooled = cot[...], pools[...]
    out = pooled.astype(F32)
    for t in range(4):
        g_out = dot(acts[t], ct, 0, 0)
        g_in = dot(pooled, gpres[t], 0, 0)
        for h in (0, 1):
            wacc[pl.ds(h * 1024 + t * 256, 256), :] = g_out[:, h * 128:(h + 1) * 128]
            wacc[pl.ds(2048 + (2 * t + h) * 256, 256), :] = g_in[:, h * 128:(h + 1) * 128]

    wstage[...] = wacc[pl.ds(2048 * (1 - k), 2048), :].astype(BF16)
    w0 = remote(wstage, wrecv0, s_w.at[0], r_w.at[0], sibling)
    w0.start()
    for t in range(4):
        out = out + dot(acts[t], wout[pl.ds(t * 256, 256), :])
    louts[...] = out.astype(BF16)
    stores = [pltpu.make_async_copy(louts, lout, sem_out.at[0])]
    stores[0].start()

    def w1_copy(n):
        return remote(
            wsend1.at[n - 1], wrecv1.at[n - 1], s_w.at[1], r_w.at[1], level(spot(n)))

    def w2_copy(n):
        return remote(
            wsend2.at[(z + n) % 8], wrecv2.at[n - 1], s_w.at[2], r_w.at[2], along(n))

    def w3_copy(n):
        return remote(wsend3, wfull.at[k, spot(0), z], s_w.at[3], r_w.at[3], along(n))

    def w4_copy(n):
        part = wfull.at[k, spot(0)]
        return remote(part, part, s_w.at[4], r_w.at[4], level(spot(n)))

    def two_cores(n):
        at = pl.multiple_of(128 * spot(n), 128)
        return wacc[pl.ds(2048 * k + at, 128), :] + wrecv0[pl.ds(at, 128), :].astype(F32)

    def w_plane():
        w0.wait_recv()

        def one(n):
            wsend1[n - 1] = two_cores(n).astype(BF16)
            w1_copy(n).start()

        each(1, 16, one)
        wsum[...] = two_cores(0)

    def w_ring():
        take(wrecv1, r_w.at[1])
        total = wsum[...]
        for n in range(15):
            total += wrecv1[n].astype(F32)
        wsum[...] = total
        wsend2[...] = total.astype(BF16).reshape(8, 16, 128)
        each(1, 8, lambda n: w2_copy(n).start())

    def w_ring_back():
        take(wrecv2, r_w.at[2])
        total = wsum[pl.ds(pl.multiple_of(16 * z, 16), 16), :]
        for n in range(7):
            total += wrecv2[n].astype(F32)
        wsend3[...] = total.astype(BF16)
        wfull[k, spot(0), z] = wsend3[...]
        each(1, 8, lambda n: w3_copy(n).start())

    def w_plane_back():
        take(wrecv2, r_w.at[3])
        each(1, 16, lambda n: w4_copy(n).start())

    part5 = wfull.at[k]
    w5 = remote(part5, part5, s_w.at[5], r_w.at[5], sibling)

    def pass_on(f):
        take(grads[f].at[pl.ds(0, 7), 0], r_g.at[f])
        gf_copy(f).start()

    def z_copy(f, d, s, p):
        part = pl.ds(0, 2) if s > 0 else pl.ds(d, 1)
        to = across[d] if s == 3 and p == 1 else ahead[d]
        return remote(
            zstage.at[f, d, s, p, part], zrecv.at[f, d, s, p, part],
            s_z.at[f], r_z.at[f, d, s, p], to)

    def x_copy(f):
        return remote(xstage.at[f], xrecv.at[f], s_z.at[f], r_y.at[f], partner)

    def term(f, p, zz, h):
        return scan[f, last_b[2 * (((xh + p) % 2) * 8 + zz % 8) + h]]

    def z_step(f, s):
        for p in (1, 0):
            for d in (0, 1):
                target = z + sign[d] * (4 - s)
                if s > 0:
                    z_copy(f, d, s - 1, p).wait_recv()
                for h in (0, 1):
                    if s == 0 and h != d:
                        continue
                    v = term(f, p, target, h)
                    if s > 1 or (s == 1 and h == d):
                        v = v + zrecv[f, d, s - 1, p, h].astype(F32)
                    zstage[f, d, s, p, h] = v.astype(BF16)
                z_copy(f, d, s, p).start()

    def back_product(f):
        gf_copy(f).wait_recv()
        aggregate(f, valt, rows, prev_b, lambda f, i: grads[f][i // 4, (i // 2) % 2, i % 2])
        z_step(f, 0)
        for h in (0, 1):
            xstage[f, h] = term(f, 1, z, h).astype(BF16)
        x_copy(f).start()

    w_plane()
    pass_on(0)
    back_product(0)
    z_step(0, 1)
    w_ring()
    z_step(0, 2)
    pass_on(1)
    back_product(1)
    w_ring_back()
    z_step(0, 3)
    z_step(1, 1)
    w_plane_back()
    z_step(1, 2)
    z_step(1, 3)

    def arrive(f):
        x_copy(f).wait_recv()
        for p in (0, 1):
            for d in (0, 1):
                z_copy(f, d, 3, p).wait_recv()
        for h in (0, 1):
            v = term(f, 0, z, h) + xrecv[f, h].astype(F32)
            for p in (0, 1):
                for d in (0, 1):
                    v = v + zrecv[f, d, 3, p, h].astype(F32)
            gxs[f, h] = v.astype(BF16)
        stores.append(pltpu.make_async_copy(gxs.at[f], gx.at[:, :, halves[f]], sem_out.at[1 + f]))
        stores[-1].start()

    arrive(0)
    take(wfull.at[k, pl.ds(0, 15)], r_w.at[4])
    w5.start()
    arrive(1)
    w5.wait_recv()
    for h in (0, 1):
        one = pltpu.make_async_copy(
            wfull.at[0, pl.ds(8 * h, 8)], gwout.at[:, :, :, halves[h]], sem_out.at[3])
        one.start()
    for t in range(8):
        one = pltpu.make_async_copy(
            wfull.at[1, pl.ds(2 * t, 2)], gwin.at[:, :, :, pl.ds(128 * t, 128)], sem_out.at[3])
        one.start()

    for one in stores:
        one.wait()
    take(wfull, sem_out.at[3])
    for f in (0, 1):
        take(feats[f].at[pl.ds(0, 30)], s_ag.at[f])
        take(feats[f].at[pl.ds(0, 30)], s_z.at[f])
        for g in (0, 1):
            p_copy(f, g).wait_send()
        take(qrecv.at[f], s_q.at[f])
        take(qrecv.at[f], s_g.at[f])
        gf_copy(f).wait_send()
    w0.wait_send()
    take(wrecv1, s_w.at[1])
    take(wrecv2, s_w.at[2])
    take(wrecv2, s_w.at[3])
    take(wfull.at[k, pl.ds(0, 15)], s_w.at[4])
    w5.wait_send()


def finish(*refs):
    inputs, outputs, here, wide, sem = refs[:4], refs[4:8], refs[8:12], refs[12:14], refs[14]
    halves = []
    for i in (2, 3, 0, 1):
        n = inputs[i].shape[0] // 2
        halves += [(i, pl.ds(n * h, n), h) for h in (0, 1)]
    ins = [
        pltpu.make_async_copy(inputs[i].at[at], here[i].at[at], sem.at[i, h]) for i, at, h in halves
    ]
    for one in ins:
        one.start()
    outs = []
    for (i, at, h), one in zip(halves, ins):
        one.wait()
        source = here[i] if i < 2 else wide[i - 2]
        if i >= 2:
            source[at] = here[i][at].astype(F32)
        outs.append(pltpu.make_async_copy(source.at[at], outputs[i].at[at], sem.at[i + 4, h]))
        outs[-1].start()
    for one in outs:
        one.wait()


def body(features, block_values, block_rows, block_cols, block_count, weight_in, weight_out, cot):
    vm = lambda *shape, t=BF16: pltpu.VMEM(shape, t)
    dma = lambda *shape: pltpu.SemaphoreType.DMA(shape)
    hbm = pl.BlockSpec(memory_space=pltpu.HBM)
    sm = lambda *shape: pltpu.SMEM(shape, jnp.int32)
    lout, gx, gwin, gwout = pl.pallas_call(
        kernel,
        out_shape=(
            jax.ShapeDtypeStruct((2 * BLK, WIDTH), BF16),
            jax.ShapeDtypeStruct((2, BLK, WIDTH), BF16),
            jax.ShapeDtypeStruct((2, 8, 16, HID), BF16),
            jax.ShapeDtypeStruct((8, 8, 16, WIDTH), BF16),
        ),
        in_specs=[hbm] * 8,
        out_specs=(hbm,) * 4,
        scratch_shapes=[
            sm(1, 1, SLOTS), sm(1, 1, SLOTS), sm(1, 1), sm(SLOTS), sm(SLOTS), sm(SLOTS), sm(SLOTS),
            vm(SLOTS, BLK, BLK), vm(SLOTS, BLK, BLK), vm(WIDTH, HID), vm(HID, WIDTH),
            vm(2 * BLK, WIDTH), vm(2 * BLK, WIDTH), vm(2, 2, BLK, HALF),
            vm(BLOCKS, BLK, HALF), vm(BLOCKS, BLK, HALF),
            vm(8, 2, 2, BLK, HALF), vm(8, 2, 2, BLK, HALF),
            vm(2, SLOTS + 1, BLK, HALF, t=F32),
            vm(2, 8, 2, BLK, HALF), vm(2, 8, 2, BLK, HALF), vm(2, 2, 7, BLK, HALF),
            vm(2, 2, 7, BLK, HALF), vm(2, 2, BLK, HALF, t=F32),
            vm(2, 2, 4, 2, 2, BLK, HALF), vm(2, 2, 4, 2, 2, BLK, HALF),
            vm(2, 2, BLK, HALF), vm(2, 2, BLK, HALF), vm(2, 2, BLK, HALF),
            vm(4, 256, 256, t=F32), vm(4, 256, 256), vm(4, 256, 256), vm(2 * BLK, WIDTH),
            vm(4096, 128, t=F32), vm(2048, 128), vm(2048, 128), vm(15, 128, 128),
            vm(15, 128, 128), vm(128, 128, t=F32), vm(8, 16, 128), vm(7, 16, 128),
            vm(16, 128), vm(2, 16, 8, 16, 128),
            dma(9), dma(4), dma(2), dma(2, 2, 4, 2), dma(2), dma(2),
            dma(2, 2), dma(2, 2), dma(2), dma(2, 2), dma(2), dma(2), dma(2), dma(2),
            dma(2), dma(2, 2, 4, 2), dma(6), dma(6),
        ],
        compiler_params=pltpu.CompilerParams(
            collective_id=0, has_side_effects=True, vmem_limit_bytes=60 * 2**20
        ),
        name="layer",
    )(
        block_rows, block_cols, block_count, features.reshape(2, BLK, WIDTH),
        block_values[0, 0], weight_in, weight_out, cot,
    )
    lout, gx, gwin, gwout = pl.pallas_call(
        finish,
        out_shape=(
            jax.ShapeDtypeStruct((2 * BLK, WIDTH), BF16),
            jax.ShapeDtypeStruct((2, BLK, WIDTH), BF16),
            jax.ShapeDtypeStruct((WIDTH, HID), F32),
            jax.ShapeDtypeStruct((HID, WIDTH), F32),
        ),
        in_specs=[hbm] * 4,
        out_specs=(hbm,) * 4,
        scratch_shapes=[
            vm(2 * BLK, WIDTH), vm(2, BLK, WIDTH), vm(WIDTH, HID), vm(HID, WIDTH),
            vm(WIDTH, HID, t=F32), vm(HID, WIDTH, t=F32), dma(8, 2),
        ],
        compiler_params=pltpu.CompilerParams(vmem_limit_bytes=60 * 2**20),
        name="finish",
    )(lout, gx, gwin.reshape(WIDTH, HID), gwout.reshape(HID, WIDTH))
    return lout, gx.reshape(2 * BLK, WIDTH), gwin, gwout


def solution(mesh):
    return jax.shard_map(
        body,
        mesh=mesh,
        in_specs=(
            P(("col", "row"), None),
            P("row", "col", None, None, None),
            P("row", "col", None),
            P("row", "col", None),
            P("row", "col"),
            P(),
            P(),
            P(("row", "col"), None),
        ),
        out_specs=(P(("row", "col"), None), P(("col", "row"), None), P(), P()),
        check_vma=False,
    )
```
